256 devices in a mesh: dp: 16 (over x, z_hi), tensor: 16 (over z_lo, y, core).
Axes of the slice: x: 4, y: 4, z: 8 (z_hi: 4, z_lo: 2; z = z_hi * 2 + z_lo), core: 2. Of those that a mesh axis runs over, the one named last changes fastest.
Arguments:
- inputs: bfloat16 [32768, 28672], P('dp', 'tensor'), may hold values from -6 to 6
- out_grads: bfloat16 [32768, 8192], P(('dp', 'tensor')), may hold values from -6 to 6
- proj_in: bfloat16 [28672, 64], P('tensor'), may hold values from -0.03125 to 0.03125
- proj_out: bfloat16 [8192, 64], replicated, may hold values from -0.0625 to 0.0625
- example_ids: int32 [16, 2048], P('dp'), may hold values from 0 to 3, never falling along the last dimension, each value on 1 to 768 neighbouring positions
Outputs:
- covariance: float32 [4096, 4096], P('dp', 'tensor')
The draws below stay inside these ranges and needn't reach their ends.
Inputs may be any that keep to these rules, and one draw needn't show every extreme that they name: `example_ids`: along each group the example number never falls; each of the 4 examples has 1 to 768 tokens and in every group one has exactly 768.
All inputs are finite; a program needn't handle non-finite values.
Results may differ from the reference program's by a relative error of at most 0.0003.
Values sent between devices are 32-bit elements; how exact they have to be, the bound alone decides.
A program may use at most 64 MiB of HBM per device.

```python
import math
from functools import partial
import jax
import jax.numpy as jnp
import numpy as np
from jax import lax

IN = 28672
OUT = 8192
RANK = 64
SEQ = 512
EX_DEV = 4
VEC = 4096
MOST = 768
TOK_GRP = 2048
GROUPS = 16
EXAMPLES = 64
TOKENS = 32768


def steps_of(stream_key, extent, pieces, low, largest):
    loudness = 1.0
    for position, parts in pieces:
        draws = jax.random.uniform(jax.random.fold_in(jax.random.fold_in(stream_key, 6), position), (parts,), jnp.float32, low / len(pieces), largest / len(pieces))
        loudness = loudness * jnp.repeat(jnp.exp(draws), extent[position] // parts).reshape((-1,) + (1,) * (len(extent) - 1 - position))
    return loudness


def profile(count, total, limit, skew):
    weights = [(1 << 20) // math.isqrt(grade ** skew) + 1 for grade in range(2, count + 1)]
    spare, counts = total - limit - (count - 1), [1] * (count - 1)
    while spare > 0:
        free = [i for i in range(count - 1) if counts[i] < limit]
        mass, budget = sum([weights[i] for i in free]), spare
        for i in free:
            extra = min(limit - counts[i], max(1, budget * weights[i] // mass), spare)
            counts[i] = counts[i] + extra
            spare = spare - extra
    return np.array([limit] + counts)


def uneven(key, number_of, total, most, slope):
    if number_of == 2:
        one = jax.random.randint(key, (), max(1, total - most), min(most, total - 1) + 1)
        return jnp.stack([one, total - one])
    sizes = jnp.asarray(profile(number_of, total, most, slope), jnp.int32)
    couples = (number_of - 1) // 2
    giver, sink = sizes[1:1 + 2 * couples:2], sizes[2:2 + 2 * couples:2]
    room = jnp.minimum(giver - 1, most - sink)
    shifted = jax.random.randint(jax.random.fold_in(key, 1), (couples,), 0, 1 << 20) % (room + 1)
    sizes = sizes.at[1:1 + 2 * couples:2].set(giver - shifted).at[2:2 + 2 * couples:2].set(sink + shifted)
    return sizes[jax.random.permutation(jax.random.fold_in(key, 2), number_of)]


def gaussian(stream_key, shape, scale, limit, cuts=(), dtype=jnp.bfloat16):
    drawn = jax.random.normal(stream_key, shape, jnp.float32) * scale
    if len(cuts) > 0:
        drawn = steps_of(stream_key, shape, cuts, -0.22, 0.18) * drawn
    return jnp.clip(drawn, min=-limit, max=limit).astype(dtype)


def setup_inputs(seed: int = 0) -> dict:
    keys = jax.random.split(jax.random.key(seed), 6)
    inputs = gaussian(keys[0], (TOKENS, IN), 1.0, 6.0, ((0, 16), (1, 16)))
    out_grads = gaussian(keys[1], (TOKENS, OUT), 1.0, 6.0, ((0, 256),))
    proj_in = gaussian(keys[2], (IN, RANK), IN ** -0.5, 0.03125, ((0, 16),))
    proj_out = gaussian(keys[3], (OUT, RANK), OUT ** -0.5, 0.0625)
    example_ids = jax.vmap(lambda own: jnp.searchsorted(jnp.cumsum(uneven(own, EX_DEV, TOK_GRP, MOST, 1)), jnp.arange(TOK_GRP), side="right"))(jax.random.split(keys[4], GROUPS)).reshape((GROUPS, TOK_GRP)).astype(jnp.int32)
    return dict(inputs=inputs, out_grads=out_grads, proj_in=proj_in, proj_out=proj_out, example_ids=example_ids)


def group_vectors(proj_in, proj_out, operands):
    group_inputs, group_grads, token_ids = operands
    input_sketch = lax.dot_general(proj_in, group_inputs, (((0,), (1,)), ((), ())), preferred_element_type=jnp.float32)
    grad_sketch = lax.dot_general(proj_out, group_grads, (((0,), (1,)), ((), ())), preferred_element_type=jnp.float32)
    labels = jnp.arange(EX_DEV).astype(jnp.int32)
    onehot = (token_ids.astype(jnp.int32)[None, :] == labels[:, None]).astype(jnp.float32)
    weighted = (input_sketch[None, :, :] * onehot[:, None, :]).reshape(EX_DEV * RANK, TOK_GRP)
    products = lax.dot_general(weighted, grad_sketch, (((1,), (1,)), ((), ())), precision=lax.Precision.HIGHEST, preferred_element_type=jnp.float32)
    return products.reshape(EX_DEV, VEC)


def reference(inputs, out_grads, proj_in, proj_out, example_ids):
    groups = example_ids.shape[0]
    grouped_inputs = inputs.reshape(groups, TOK_GRP, IN)
    grouped_grads = out_grads.reshape(groups, TOK_GRP, OUT)
    vectors = lax.map(partial(group_vectors, proj_in, proj_out), (grouped_inputs, grouped_grads, example_ids))
    vectors = vectors.reshape(EXAMPLES, VEC)
    product = jnp.dot(vectors.T, vectors, precision=lax.Precision.HIGHEST, preferred_element_type=jnp.float32)
    return product / (EXAMPLES * SEQ)
```

```python
import jax
import jax.numpy as jnp
from jax import lax
from jax.experimental import pallas as pl
from jax.experimental.pallas import tpu as pltpu
from jax.sharding import PartitionSpec as P

SEQ = 512
EX_DEV = 4
MESH = pl.DeviceIdType.MESH
F32 = jnp.float32
BF16 = jnp.bfloat16
NT = (((1,), (1,)), ((), ()))


def split(x):
    high = x.astype(BF16)
    return high, (x - high.astype(F32)).astype(BF16)


def kernel(
    x_hbm, og_hbm, wi_hbm, wo_hbm, ids_hbm, out_ref,
    x_v, og_v, wi_v, wo_v, ids_v, g_v, give, take, masked, pieces, shares, mine, cols, rows,
    local_sem, x_sem, g_send, g_recv, s_send, s_recv, b_send, b_recv, c_send, col_recv, row_recv,
):
    dp = lax.axis_index("dp")
    tensor = lax.axis_index("tensor")
    core = lax.rem(tensor, 2)
    chip = lax.div(tensor, 2)
    partner = (dp, tensor + 1 - 2 * core)

    og_copy = pltpu.make_async_copy(og_hbm, og_v, local_sem.at[0])
    wo_copy = pltpu.make_async_copy(wo_hbm, wo_v, local_sem.at[1])
    wi_copy = pltpu.make_async_copy(wi_hbm, wi_v, local_sem.at[2])
    ids_copy = pltpu.make_async_copy(ids_hbm, ids_v, local_sem.at[3])
    wo_copy.start()
    og_copy.start()
    wi_copy.start()
    ids_copy.start()
    x_copies = []
    for half in range(2):
        parity = (1 - core) if half == 0 else core
        for b in range(8):
            slot = half * 8 + b
            copy = pltpu.make_async_copy(
                x_hbm.at[pl.ds(pl.multiple_of((2 * b + parity) * 128, 128), 128), :],
                x_v.at[slot],
                x_sem.at[slot],
            )
            copy.start()
            x_copies.append(copy)

    barrier = pltpu.get_barrier_semaphore()

    def greet(rel, carry):
        pl.semaphore_signal(barrier, inc=1, device_id=(dp, lax.rem(tensor + rel, 16)), device_id_type=MESH)
        pl.semaphore_signal(barrier, inc=1, device_id=(lax.rem(dp + rel, 16), tensor), device_id_type=MESH)
        pl.semaphore_signal(barrier, inc=1, device_id=(lax.rem(dp + rel, 16), dp), device_id_type=MESH)
        return carry

    lax.fori_loop(1, 16, greet, 0)

    @pl.when(tensor != dp)
    def _():
        pl.semaphore_signal(barrier, inc=1, device_id=(dp, dp), device_id_type=MESH)

    wo_copy.wait()
    og_copy.wait()
    g_v[chip] = lax.dot_general(wo_v[...], og_v[...], NT, preferred_element_type=F32)

    pl.semaphore_wait(barrier, jnp.where(tensor == dp, 45, 46))

    g_copies = []
    for rel in range(1, 8):
        peer = lax.rem(chip + rel, 8)
        copy = pltpu.make_async_remote_copy(
            src_ref=g_v.at[chip], dst_ref=g_v.at[chip], send_sem=g_send.at[rel], recv_sem=g_recv.at[rel],
            device_id=(dp, 2 * peer + core), device_id_type=MESH,
        )
        copy.start()
        g_copies.append(copy)

    wi_copy.wait()
    ids_copy.wait()
    s_copies = []
    for pair in range(4):
        x_copies[2 * pair].wait()
        x_copies[2 * pair + 1].wait()
        block = x_v[2 * pair : 2 * pair + 2].reshape(256, 1792)
        sketch = lax.dot_general(wi_v[...], block, NT, preferred_element_type=F32)
        give[2 * pair] = sketch[:, :128]
        give[2 * pair + 1] = sketch[:, 128:]
        copy = pltpu.make_async_remote_copy(
            src_ref=give.at[pl.ds(2 * pair, 2)], dst_ref=take.at[pl.ds(2 * pair, 2)],
            send_sem=s_send.at[pair], recv_sem=s_recv.at[pair], device_id=partner, device_id_type=MESH,
        )
        copy.start()
        s_copies.append(copy)
    for pair in range(4):
        x_copies[8 + 2 * pair].wait()
        x_copies[8 + 2 * pair + 1].wait()
        block = x_v[8 + 2 * pair : 8 + 2 * pair + 2].reshape(256, 1792)
        sketch = lax.dot_general(wi_v[...], block, NT, preferred_element_type=F32)
        s_copies[pair].wait_recv()
        for k in range(2):
            b = 2 * pair + k
            total = sketch[:, 128 * k : 128 * (k + 1)] + take[b]
            ids = ids_v[:, pl.ds(pl.multiple_of((2 * b + core) * 128, 128), 128)]
            high, low = split(total)
            for e in range(EX_DEV):
                own = ids == e
                lanes = slice(128 * b, 128 * (b + 1))
                masked[64 * e : 64 * (e + 1), lanes] = jnp.where(own, high, jnp.zeros_like(high))
                masked[256 + 64 * e : 256 + 64 * (e + 1), lanes] = jnp.where(own, low, jnp.zeros_like(low))

    for copy in g_copies:
        copy.wait_recv()
    grads = []
    for b in range(8):
        high, low = split(g_v[b])
        grads.append(jnp.concatenate([high, low], axis=0))
    product = lax.dot_general(
        masked[...], jnp.concatenate(grads, axis=1), NT, preferred_element_type=F32
    )
    lane = lax.broadcasted_iota(jnp.int32, (64, 128), 1)
    both = []
    for e in range(EX_DEV):
        term = product[64 * e : 64 * (e + 1)] + product[256 + 64 * e : 256 + 64 * (e + 1)]
        both.append(term + pltpu.roll(term, 64, 1))
    first = jnp.where(lane < 64, both[0], both[1]).reshape(8, 8, 128)
    second = jnp.where(lane < 64, both[2], both[3]).reshape(8, 8, 128)
    row8 = lax.broadcasted_iota(jnp.int32, (8, 8, 128), 1)
    even = jnp.where(row8 < 4, first, pltpu.roll(second, 4, 1))
    odd = jnp.where(row8 < 4, pltpu.roll(first, 4, 1), second)
    for u in range(8):
        pieces[2 * u] = even[u]
        pieces[2 * u + 1] = odd[u]

    shares[tensor] = pieces[tensor]
    b_copies = []
    for rel in range(1, 16):
        peer = lax.rem(tensor + rel, 16)
        copy = pltpu.make_async_remote_copy(
            src_ref=pieces.at[peer], dst_ref=shares.at[tensor], send_sem=b_send.at[rel], recv_sem=b_recv.at[rel],
            device_id=(dp, peer), device_id_type=MESH,
        )
        copy.start()
        b_copies.append(copy)
    for copy in b_copies:
        copy.wait_recv()
    total = shares[0]
    for k in range(1, 16):
        total = total + shares[k]
    row = lax.broadcasted_iota(jnp.int32, (8, 128), 0) % 2
    side = lax.broadcasted_iota(jnp.int32, (8, 128), 1) // 64
    swapped = pltpu.roll(total, 64, 1)
    piece = jnp.where(
        row == side, total, jnp.where(row == 0, pltpu.roll(swapped, 7, 0), pltpu.roll(swapped, 1, 0))
    )
    mine[...] = piece

    cols[dp] = piece

    c_copies = []
    for rel in range(1, 16):
        copy = pltpu.make_async_remote_copy(
            src_ref=mine, dst_ref=cols.at[dp], send_sem=c_send.at[rel], recv_sem=col_recv.at[rel],
            device_id=(lax.rem(dp + rel, 16), tensor), device_id_type=MESH,
        )
        copy.start()
        c_copies.append(copy)
    row_copies = []
    for rel in range(1, 16):
        copy = pltpu.make_async_remote_copy(
            src_ref=mine, dst_ref=rows.at[dp], send_sem=c_send.at[16 + rel], recv_sem=row_recv.at[dp],
            device_id=(tensor, lax.rem(dp + rel, 16)), device_id_type=MESH,
        )
        copy.start()
        row_copies.append(copy)
    last = pltpu.make_async_remote_copy(
        src_ref=mine, dst_ref=rows.at[dp], send_sem=c_send.at[16], recv_sem=row_recv.at[dp],
        device_id=(tensor, dp), device_id_type=MESH,
    )

    @pl.when(tensor != dp)
    def _():
        last.start()

    @pl.when(tensor == dp)
    def _():
        rows[dp] = piece

    for copy in c_copies:
        copy.wait_recv()
    for g in range(16):
        @pl.when(jnp.logical_or(tensor != dp, dp != g))
        def _():
            pltpu.make_async_copy(rows.at[g], rows.at[g], row_recv.at[g]).wait()

    r2 = rows[...].reshape(128, 128).T
    c2 = cols[...].reshape(128, 128)
    r_bit = (lax.broadcasted_iota(jnp.int32, (128, 128), 1) // 2) % 2
    c_bit = (lax.broadcasted_iota(jnp.int32, (128, 128), 0) // 2) % 2
    zero = jnp.zeros_like(r2)
    left = jnp.concatenate([jnp.where(r_bit == 0, r2, zero), jnp.where(r_bit == 1, r2, zero)], axis=0)
    right = jnp.concatenate(
        [jnp.where(c_bit == 0, c2, pltpu.roll(c2, 2, 0)), jnp.where(c_bit == 1, c2, pltpu.roll(c2, 126, 0))], axis=1
    )
    lh, ll = split(left)
    rh, rl = split(right)
    dot = lambda a, b: jnp.dot(a, b, preferred_element_type=F32)
    out_ref[...] = (dot(lh, rl) + dot(ll, rh) + dot(lh, rh)) * (1.0 / (64 * SEQ))

    for copy in g_copies + s_copies + b_copies + c_copies + row_copies:
        copy.wait_send()

    @pl.when(tensor != dp)
    def _():
        last.wait_send()


def per_device(inputs, out_grads, proj_in, proj_out, example_ids):
    any_space = pl.BlockSpec(memory_space=pl.ANY)
    dma = pltpu.SemaphoreType.DMA
    return pl.pallas_call(
        kernel,
        out_shape=jax.ShapeDtypeStruct((256, 256), F32),
        in_specs=[any_space] * 5,
        out_specs=pl.BlockSpec(memory_space=pltpu.VMEM),
        scratch_shapes=[
            pltpu.VMEM((16, 128, 1792), BF16),
            pltpu.VMEM((128, 8192), BF16),
            pltpu.VMEM((64, 1792), BF16),
            pltpu.VMEM((64, 8192), BF16),
            pltpu.VMEM((1, 2048), jnp.int32),
            pltpu.VMEM((8, 64, 128), F32),
            pltpu.VMEM((8, 64, 128), F32),
            pltpu.VMEM((8, 64, 128), F32),
            pltpu.VMEM((512, 1024), BF16),
            pltpu.VMEM((16, 8, 128), F32),
            pltpu.VMEM((16, 8, 128), F32),
            pltpu.VMEM((8, 128), F32),
            pltpu.VMEM((16, 8, 128), F32),
            pltpu.VMEM((16, 8, 128), F32),
            dma((4,)), dma((16,)), dma((8,)), dma((8,)), dma((4,)), dma((4,)),
            dma((16,)), dma((16,)), dma((32,)), dma((16,)), dma((16,)),
        ],
        compiler_params=pltpu.CompilerParams(
            collective_id=0, has_side_effects=True, vmem_limit_bytes=48 * 1024 * 1024
        ),
        cost_estimate=pl.CostEstimate(flops=10**9, bytes_accessed=12 * 10**6, transcendentals=0),
    )(inputs, out_grads, proj_in.T, proj_out.T, example_ids)


def solution(mesh):
    placed = (P("dp", "tensor"), P(("dp", "tensor"), None), P("tensor", None), P(), P("dp", None))
    return jax.shard_map(
        per_device, mesh=mesh, in_specs=placed, out_specs=P("dp", "tensor"), check_vma=False
    )
```

```python
import jax
import jax.numpy as jnp
from jax import lax
from jax.experimental import pallas as pl
from jax.experimental.pallas import tpu as pltpu
from jax.sharding import PartitionSpec as P

SEQ = 512
EX_DEV = 4
MESH = pl.DeviceIdType.MESH
F32 = jnp.float32
BF16 = jnp.bfloat16
NT = (((1,), (1,)), ((), ()))

CHIPS = (6, 5, 7, 2, 4, 1, 3)
TENSORS = (12, 13, 10, 11, 14, 15, 4, 5, 8, 9, 2, 3, 6, 7, 1)
GROUPS = (10, 6, 14, 2, 9, 11, 5, 7, 13, 15, 1, 3, 8, 4, 12)


def split(x):
    high = x.astype(BF16)
    return high, (x - high.astype(F32)).astype(BF16)


def kernel(
    x_hbm, og_hbm, wi_hbm, wo_hbm, ids_hbm, out_ref,
    x_v, og_v, wi_v, wo_v, ids_v, g_v, give, take, masked, pieces, shares, mine, cols, rows,
    local_sem, x_sem, g_send, g_recv, s_send, s_recv, b_send, b_recv, c_send, last_send, col_recv, row_recv,
    x_known, z_known, all_known,
):
    dp = lax.axis_index("dp")
    tensor = lax.axis_index("tensor")
    core = lax.rem(tensor, 2)
    chip = lax.div(tensor, 2)
    y = lax.rem(chip, 4)
    z = lax.div(chip, 4)
    partner = (dp, lax.bitwise_xor(tensor, 1))

    g_reads = []
    for k in range(2):
        half = pl.ds(4096 * k, 4096)
        pair = (
            pltpu.make_async_copy(wo_hbm.at[:, half], wo_v.at[:, half], local_sem.at[2 * k]),
            pltpu.make_async_copy(og_hbm.at[:, half], og_v.at[:, half], local_sem.at[2 * k + 1]),
        )
        for copy in pair:
            copy.start()
        g_reads.append(pair)
    wi_copy = pltpu.make_async_copy(wi_hbm, wi_v, local_sem.at[4])
    ids_copy = pltpu.make_async_copy(ids_hbm, ids_v, local_sem.at[5])
    x_copies = []
    for part in range(4):
        side = lax.bitwise_xor(z, part % 2)
        owner = 1 - core if part < 2 else core
        x_copies.append(pltpu.make_async_copy(x_hbm.at[side, :, owner], x_v.at[part], x_sem.at[part]))

    barrier = pltpu.get_barrier_semaphore()
    x_peers = [(lax.bitwise_xor(dp, 4 * r), tensor) for r in (2, 1, 3)]
    z_peers = [(lax.bitwise_xor(dp, r), tensor) for r in (1, 3)]
    near = [(dp, lax.bitwise_xor(tensor, r)) for r in TENSORS] + x_peers + z_peers
    for peer in near:
        pl.semaphore_signal(barrier, inc=1, device_id=peer, device_id_type=MESH)

    sketch = []
    for k in range(2):
        for copy in g_reads[k]:
            copy.wait()
        if k == 1:
            wi_copy.start()
            ids_copy.start()
            x_copies[0].start()
            x_copies[1].start()
        half = slice(4096 * k, 4096 * (k + 1))
        sketch.append(lax.dot_general(og_v[:, half], wo_v[:, half], NT, preferred_element_type=F32))
    g_v[y] = (sketch[0] + sketch[1]).T

    pl.semaphore_wait(barrier, len(near))
    g_copies = []
    for r in CHIPS:
        copy = pltpu.make_async_remote_copy(
            src_ref=g_v.at[y], dst_ref=g_v.at[4 * (r // 4) + y],
            send_sem=g_send, recv_sem=g_recv.at[r // 4],
            device_id=(dp, 2 * lax.bitwise_xor(chip, r) + core), device_id_type=MESH,
        )
        copy.start()
        g_copies.append(copy)
    for peer in x_peers:
        pl.semaphore_signal(x_known, inc=1, device_id=peer, device_id_type=MESH)

    wi_copy.wait()
    ids_copy.wait()
    s_copies = []
    for part in range(4):
        x_copies[part].wait()
        if part < 2:
            x_copies[part + 2].start()
        sketch = lax.dot_general(
            wi_v[...], x_v[part].reshape(512, 1792), NT, preferred_element_type=F32
        )
        if part < 2:
            give[part] = sketch
            copy = pltpu.make_async_remote_copy(
                src_ref=give.at[part], dst_ref=take.at[part],
                send_sem=s_send.at[part], recv_sem=s_recv.at[part], device_id=partner, device_id_type=MESH,
            )
            copy.start()
            s_copies.append(copy)
            continue
        s_copies[part - 2].wait_recv()
        total = sketch + take[part - 2]
        side = lax.bitwise_xor(z, part % 2)
        ids = jnp.concatenate(
            [ids_v[:, pl.ds(pl.multiple_of((8 * side + 2 * b + core) * 128, 128), 128)] for b in range(4)], axis=1
        )
        high, low = split(total)
        lanes = slice(512 * (part - 2), 512 * (part - 1))
        for e in range(EX_DEV):
            own = ids == e
            masked[64 * e : 64 * (e + 1), lanes] = jnp.where(own, high, jnp.zeros_like(high))
            masked[256 + 64 * e : 256 + 64 * (e + 1), lanes] = jnp.where(own, low, jnp.zeros_like(low))

    pl.semaphore_wait(x_known, len(x_peers))
    for peer in z_peers:
        pl.semaphore_signal(z_known, inc=1, device_id=peer, device_id_type=MESH)

    product = None
    for side in range(2):
        count = 3 if side == 0 else 4
        arrived = g_v.at[pl.ds(0, count)]
        pltpu.make_async_copy(arrived, arrived, g_recv.at[side]).wait()
        grads = []
        for b in range(4):
            high, low = split(g_v[4 * side + b])
            grads.append(jnp.concatenate([high, low], axis=0))
        term = lax.dot_general(
            masked[:, 512 * side : 512 * (side + 1)], jnp.concatenate(grads, axis=1), NT, preferred_element_type=F32
        )
        product = term if side == 0 else product + term
    lane = lax.broadcasted_iota(jnp.int32, (64, 128), 1)
    both = []
    for e in range(EX_DEV):
        term = product[64 * e : 64 * (e + 1)] + product[256 + 64 * e : 256 + 64 * (e + 1)]
        both.append(term + pltpu.roll(term, 64, 1))
    first = jnp.where(lane < 64, both[0], both[1]).reshape(8, 8, 128)
    second = jnp.where(lane < 64, both[2], both[3]).reshape(8, 8, 128)
    row8 = lax.broadcasted_iota(jnp.int32, (8, 8, 128), 1)
    even = jnp.where(row8 < 4, first, pltpu.roll(second, 4, 1))
    odd = jnp.where(row8 < 4, pltpu.roll(first, 4, 1), second)
    for u in range(8):
        pieces[2 * u] = even[u]
        pieces[2 * u + 1] = odd[u]

    for r in TENSORS:
        peer = lax.bitwise_xor(tensor, r)
        pltpu.make_async_remote_copy(
            src_ref=pieces.at[peer], dst_ref=shares.at[r], send_sem=b_send, recv_sem=b_recv,
            device_id=(dp, peer), device_id_type=MESH,
        ).start()
    pl.semaphore_wait(z_known, len(z_peers))
    for peer in z_peers:
        pl.semaphore_signal(all_known, inc=1, device_id=peer, device_id_type=MESH)
    shares[0] = pieces[tensor]
    pl.semaphore_wait(all_known, len(z_peers))
    others = shares.at[pl.ds(1, 15)]
    pltpu.make_async_copy(others, others, b_recv).wait()
    total = shares[0]
    for k in range(1, 16):
        total = total + shares[k]
    row = lax.broadcasted_iota(jnp.int32, (8, 128), 0) % 2
    lane_half = lax.broadcasted_iota(jnp.int32, (8, 128), 1) // 64
    swapped = pltpu.roll(total, 64, 1)
    piece = jnp.where(
        row == lane_half, total, jnp.where(row == 0, pltpu.roll(swapped, 7, 0), pltpu.roll(swapped, 1, 0))
    )
    mine[...] = piece

    for r in TENSORS:
        pltpu.make_async_remote_copy(
            src_ref=mine, dst_ref=rows.at[dp], send_sem=c_send, recv_sem=row_recv,
            device_id=(tensor, lax.bitwise_xor(tensor, r)), device_id_type=MESH,
        ).start()
    for r in GROUPS:
        pltpu.make_async_remote_copy(
            src_ref=mine, dst_ref=cols.at[dp], send_sem=c_send, recv_sem=col_recv,
            device_id=(lax.bitwise_xor(dp, r), tensor), device_id_type=MESH,
        ).start()
    last = pltpu.make_async_remote_copy(
        src_ref=mine, dst_ref=rows.at[dp], send_sem=last_send, recv_sem=row_recv,
        device_id=(tensor, tensor), device_id_type=MESH,
    )
    here = pltpu.make_async_copy(mine, rows.at[dp], row_recv)

    @pl.when(tensor != dp)
    def _():
        last.start()

    @pl.when(tensor == dp)
    def _():
        here.start()

    cols[dp] = piece
    others = cols.at[pl.ds(0, 15)]
    pltpu.make_async_copy(others, others, col_recv).wait()
    pltpu.make_async_copy(rows, rows, row_recv).wait()

    r2 = rows[...].reshape(128, 128).T
    c2 = cols[...].reshape(128, 128)
    r_bit = (lax.broadcasted_iota(jnp.int32, (128, 128), 1) // 2) % 2
    c_bit = (lax.broadcasted_iota(jnp.int32, (128, 128), 0) // 2) % 2
    zero = jnp.zeros_like(r2)
    left = jnp.concatenate([jnp.where(r_bit == 0, r2, zero), jnp.where(r_bit == 1, r2, zero)], axis=0)
    right = jnp.concatenate(
        [jnp.where(c_bit == 0, c2, pltpu.roll(c2, 2, 0)), jnp.where(c_bit == 1, c2, pltpu.roll(c2, 126, 0))], axis=1
    )
    lh, ll = split(left)
    rh, rl = split(right)
    dot = lambda a, b: jnp.dot(a, b, preferred_element_type=F32)
    out_ref[...] = (dot(lh, rl) + dot(ll, rh) + dot(lh, rh)) * (1.0 / (64 * SEQ))

    for copy in s_copies:
        copy.wait_send()
    sent = g_v.at[pl.ds(0, 7)]
    pltpu.make_async_copy(sent, sent, g_send).wait()
    sent = shares.at[pl.ds(0, 15)]
    pltpu.make_async_copy(sent, sent, b_send).wait()
    sent = cols.at[pl.ds(0, 15)]
    pltpu.make_async_copy(sent, sent, c_send).wait()
    pltpu.make_async_copy(sent, sent, c_send).wait()

    @pl.when(tensor != dp)
    def _():
        last.wait_send()


def per_device(inputs, out_grads, proj_in, proj_out, example_ids):
    hbm = pl.BlockSpec(memory_space=pltpu.HBM)
    dma = pltpu.SemaphoreType.DMA
    regular = pltpu.SemaphoreType.REGULAR
    return pl.pallas_call(
        kernel,
        out_shape=jax.ShapeDtypeStruct((256, 256), F32),
        in_specs=[hbm] * 5,
        out_specs=pl.BlockSpec(memory_space=pltpu.VMEM),
        scratch_shapes=[
            pltpu.VMEM((4, 4, 128, 1792), BF16),
            pltpu.VMEM((128, 8192), BF16),
            pltpu.VMEM((64, 1792), BF16),
            pltpu.VMEM((64, 8192), BF16),
            pltpu.VMEM((1, 2048), jnp.int32),
            pltpu.VMEM((8, 64, 128), F32),
            pltpu.VMEM((2, 64, 512), F32),
            pltpu.VMEM((2, 64, 512), F32),
            pltpu.VMEM((512, 1024), BF16),
            pltpu.VMEM((16, 8, 128), F32),
            pltpu.VMEM((16, 8, 128), F32),
            pltpu.VMEM((8, 128), F32),
            pltpu.VMEM((16, 8, 128), F32),
            pltpu.VMEM((16, 8, 128), F32),
            dma((6,)), dma((4,)), dma, dma((2,)), dma((2,)), dma((2,)),
            dma, dma, dma, dma, dma, dma,
            regular, regular, regular,
        ],
        compiler_params=pltpu.CompilerParams(
            collective_id=0, has_side_effects=True, vmem_limit_bytes=57 * 1024 * 1024
        ),
        cost_estimate=pl.CostEstimate(flops=10**9, bytes_accessed=12 * 10**6, transcendentals=0),
    )(inputs.reshape(2, 4, 2, 128, 1792), out_grads, proj_in.T, proj_out.T, example_ids)


def solution(mesh):
    placed = (P("dp", "tensor"), P(("dp", "tensor"), None), P("tensor", None), P(), P("dp", None))
    return jax.shard_map(
        per_device, mesh=mesh, in_specs=placed, out_specs=P("dp", "tensor"), check_vma=False
    )
```

```python
import jax
import jax.numpy as jnp
from jax import lax
from jax.experimental import pallas as pl
from jax.experimental.pallas import tpu as pltpu
from jax.sharding import PartitionSpec as P

SEQ = 512
EX_DEV = 4
MESH = pl.DeviceIdType.MESH
F32 = jnp.float32
BF16 = jnp.bfloat16
NT = (((1,), (1,)), ((), ()))

CHIPS = (6, 5, 7, 2, 4, 1, 3)
TENSORS = (12, 13, 10, 11, 14, 15, 4, 5, 8, 9, 2, 3, 6, 7, 1)
GROUPS = (10, 6, 14, 2, 9, 11, 5, 7, 13, 15, 1, 3, 8, 4, 12)


def split(x):
    high = x.astype(BF16)
    return high, (x - high.astype(F32)).astype(BF16)


def kernel(
    x_hbm, og_hbm, wi_hbm, wo_hbm, ids_hbm, out_ref,
    x_v, og_v, wi_v, wo_v, ids_v, g_v, give, take, masked, pieces, shares, mine, cols, rows,
    local_sem, x_sem, g_send, g_recv, s_send, s_recv, b_send, b_recv, c_send, last_send, col_recv, row_recv,
    x_known, z_known, all_known,
):
    dp = lax.axis_index("dp")
    tensor = lax.axis_index("tensor")
    core = lax.rem(tensor, 2)
    chip = lax.div(tensor, 2)
    y = lax.rem(chip, 4)
    z = lax.div(chip, 4)
    partner = (dp, lax.bitwise_xor(tensor, 1))

    g_reads = []
    for k in range(2):
        half = pl.ds(4096 * k, 4096)
        pair = (
            pltpu.make_async_copy(wo_hbm.at[:, half], wo_v.at[:, half], local_sem.at[2 * k]),
            pltpu.make_async_copy(og_hbm.at[:, half], og_v.at[:, half], local_sem.at[2 * k + 1]),
        )
        for copy in pair:
            copy.start()
        g_reads.append(pair)
    wi_copy = pltpu.make_async_copy(wi_hbm, wi_v, local_sem.at[4])
    ids_copy = pltpu.make_async_copy(ids_hbm, ids_v, local_sem.at[5])
    x_copies = []
    for part in range(4):
        side = lax.bitwise_xor(z, part % 2)
        owner = 1 - core if part < 2 else core
        x_copies.append(pltpu.make_async_copy(x_hbm.at[side, :, owner], x_v.at[part], x_sem.at[part]))

    barrier = pltpu.get_barrier_semaphore()
    x_peers = [(lax.bitwise_xor(dp, 4 * r), tensor) for r in (2, 1, 3)]
    z_peers = [(lax.bitwise_xor(dp, r), tensor) for r in (1, 3)]
    near = [(dp, lax.bitwise_xor(tensor, r)) for r in TENSORS] + x_peers + z_peers
    for peer in near:
        pl.semaphore_signal(barrier, inc=1, device_id=peer, device_id_type=MESH)

    sketch = []
    for k in range(2):
        for copy in g_reads[k]:
            copy.wait()
        if k == 1:
            wi_copy.start()
            ids_copy.start()
            x_copies[0].start()
            x_copies[1].start()
        half = slice(4096 * k, 4096 * (k + 1))
        sketch.append(lax.dot_general(og_v[:, half], wo_v[:, half], NT, preferred_element_type=F32))
    g_v[y] = (sketch[0] + sketch[1]).T

    pl.semaphore_wait(barrier, len(near))
    g_copies = []
    for r in CHIPS:
        copy = pltpu.make_async_remote_copy(
            src_ref=g_v.at[y], dst_ref=g_v.at[4 * (r // 4) + y],
            send_sem=g_send, recv_sem=g_recv.at[r // 4],
            device_id=(dp, 2 * lax.bitwise_xor(chip, r) + core), device_id_type=MESH,
        )
        copy.start()
        g_copies.append(copy)
    for peer in x_peers:
        pl.semaphore_signal(x_known, inc=1, device_id=peer, device_id_type=MESH)

    wi_copy.wait()
    ids_copy.wait()
    s_copies = []
    for part in range(4):
        x_copies[part].wait()
        if part < 2:
            x_copies[part + 2].start()
        sketch = lax.dot_general(
            wi_v[...], x_v[part].reshape(512, 1792), NT, preferred_element_type=F32
        )
        if part < 2:
            give[part] = sketch
            copy = pltpu.make_async_remote_copy(
                src_ref=give.at[part], dst_ref=take.at[part],
                send_sem=s_send.at[part], recv_sem=s_recv.at[part], device_id=partner, device_id_type=MESH,
            )
            copy.start()
            s_copies.append(copy)
            continue
        s_copies[part - 2].wait_recv()
        total = sketch + take[part - 2]
        side = lax.bitwise_xor(z, part % 2)
        ids = jnp.concatenate(
            [ids_v[:, pl.ds(pl.multiple_of((8 * side + 2 * b + core) * 128, 128), 128)] for b in range(4)], axis=1
        )
        high, low = split(total)
        lanes = slice(512 * (part - 2), 512 * (part - 1))
        for e in range(EX_DEV):
            own = ids == e
            masked[64 * e : 64 * (e + 1), lanes] = jnp.where(own, high, jnp.zeros_like(high))
            masked[256 + 64 * e : 256 + 64 * (e + 1), lanes] = jnp.where(own, low, jnp.zeros_like(low))

    pl.semaphore_wait(x_known, len(x_peers))
    for peer in z_peers:
        pl.semaphore_signal(z_known, inc=1, device_id=peer, device_id_type=MESH)

    product = None
    for side in range(2):
        count = 3 if side == 0 else 4
        arrived = g_v.at[pl.ds(0, count)]
        pltpu.make_async_copy(arrived, arrived, g_recv.at[side]).wait()
        grads = []
        for b in range(4):
            high, low = split(g_v[4 * side + b])
            grads.append(jnp.concatenate([high, low], axis=0))
        term = lax.dot_general(
            masked[:, 512 * side : 512 * (side + 1)], jnp.concatenate(grads, axis=1), NT, preferred_element_type=F32
        )
        product = term if side == 0 else product + term
    lane = lax.broadcasted_iota(jnp.int32, (64, 128), 1)
    both = []
    for e in range(EX_DEV):
        term = product[64 * e : 64 * (e + 1)] + product[256 + 64 * e : 256 + 64 * (e + 1)]
        both.append(term + pltpu.roll(term, 64, 1))
    first = jnp.where(lane < 64, both[0], both[1]).reshape(8, 8, 128)
    second = jnp.where(lane < 64, both[2], both[3]).reshape(8, 8, 128)
    row8 = lax.broadcasted_iota(jnp.int32, (8, 8, 128), 1)
    even = jnp.where(row8 < 4, first, pltpu.roll(second, 4, 1))
    odd = jnp.where(row8 < 4, pltpu.roll(first, 4, 1), second)
    for u in range(8):
        pieces[2 * u] = even[u]
        pieces[2 * u + 1] = odd[u]

    for r in TENSORS:
        peer = lax.bitwise_xor(tensor, r)
        pltpu.make_async_remote_copy(
            src_ref=pieces.at[peer], dst_ref=shares.at[r], send_sem=b_send, recv_sem=b_recv,
            device_id=(dp, peer), device_id_type=MESH,
        ).start()
    pl.semaphore_wait(z_known, len(z_peers))
    for peer in z_peers:
        pl.semaphore_signal(all_known, inc=1, device_id=peer, device_id_type=MESH)
    shares[0] = pieces[tensor]
    pl.semaphore_wait(all_known, len(z_peers))
    others = shares.at[pl.ds(1, 15)]
    pltpu.make_async_copy(others, others, b_recv).wait()
    total = shares[0]
    for k in range(1, 16):
        total = total + shares[k]
    row = lax.broadcasted_iota(jnp.int32, (8, 128), 0) % 2
    lane_half = lax.broadcasted_iota(jnp.int32, (8, 128), 1) // 64
    swapped = pltpu.roll(total, 64, 1)
    piece = jnp.where(
        row == lane_half, total, jnp.where(row == 0, pltpu.roll(swapped, 7, 0), pltpu.roll(swapped, 1, 0))
    )
    mine[...] = piece

    for r in TENSORS:
        pltpu.make_async_remote_copy(
            src_ref=mine, dst_ref=rows.at[dp], send_sem=c_send, recv_sem=row_recv,
            device_id=(tensor, lax.bitwise_xor(tensor, r)), device_id_type=MESH,
        ).start()
    for r in GROUPS:
        pltpu.make_async_remote_copy(
            src_ref=mine, dst_ref=cols.at[dp], send_sem=c_send, recv_sem=col_recv,
            device_id=(lax.bitwise_xor(dp, r), tensor), device_id_type=MESH,
        ).start()
    last = pltpu.make_async_remote_copy(
        src_ref=mine, dst_ref=rows.at[dp], send_sem=last_send, recv_sem=row_recv,
        device_id=(tensor, tensor), device_id_type=MESH,
    )
    here = pltpu.make_async_copy(mine, rows.at[dp], row_recv)

    @pl.when(tensor != dp)
    def _():
        last.start()

    @pl.when(tensor == dp)
    def _():
        here.start()

    cols[dp] = piece
    others = cols.at[pl.ds(0, 15)]
    pltpu.make_async_copy(others, others, col_recv).wait()
    pltpu.make_async_copy(rows, rows, row_recv).wait()

    r2 = rows[...].reshape(128, 128).T
    c2 = cols[...].reshape(128, 128)
    r_bit = (lax.broadcasted_iota(jnp.int32, (128, 128), 1) // 2) % 2
    c_bit = (lax.broadcasted_iota(jnp.int32, (128, 128), 0) // 2) % 2
    zero = jnp.zeros_like(r2)
    left = jnp.concatenate([jnp.where(r_bit == 0, r2, zero), jnp.where(r_bit == 1, r2, zero)], axis=0)
    right = jnp.concatenate(
        [jnp.where(c_bit == 0, c2, pltpu.roll(c2, 2, 0)), jnp.where(c_bit == 1, c2, pltpu.roll(c2, 126, 0))], axis=1
    )
    lh, ll = split(left)
    rh, rl = split(right)
    dot = lambda a, b: jnp.dot(a, b, preferred_element_type=F32)
    out_ref[...] = (dot(lh, rl) + dot(ll, rh) + dot(lh, rh)) * (1.0 / (64 * SEQ))

    for copy in s_copies:
        copy.wait_send()
    sent = g_v.at[pl.ds(0, 7)]
    pltpu.make_async_copy(sent, sent, g_send).wait()
    sent = shares.at[pl.ds(0, 15)]
    pltpu.make_async_copy(sent, sent, b_send).wait()
    sent = cols.at[pl.ds(0, 15)]
    pltpu.make_async_copy(sent, sent, c_send).wait()
    pltpu.make_async_copy(sent, sent, c_send).wait()

    @pl.when(tensor != dp)
    def _():
        last.wait_send()


def per_device(inputs, out_grads, proj_in, proj_out, example_ids):
    hbm = pl.BlockSpec(memory_space=pltpu.HBM)
    dma = pltpu.SemaphoreType.DMA
    regular = pltpu.SemaphoreType.REGULAR
    return pl.pallas_call(
        kernel,
        out_shape=pltpu.VMEM((256, 256), F32),
        in_specs=[hbm] * 5,
        out_specs=pl.BlockSpec(memory_space=pltpu.VMEM),
        scratch_shapes=[
            pltpu.VMEM((4, 4, 128, 1792), BF16),
            pltpu.VMEM((128, 8192), BF16),
            pltpu.VMEM((64, 1792), BF16),
            pltpu.VMEM((64, 8192), BF16),
            pltpu.VMEM((1, 2048), jnp.int32),
            pltpu.VMEM((8, 64, 128), F32),
            pltpu.VMEM((2, 64, 512), F32),
            pltpu.VMEM((2, 64, 512), F32),
            pltpu.VMEM((512, 1024), BF16),
            pltpu.VMEM((16, 8, 128), F32),
            pltpu.VMEM((16, 8, 128), F32),
            pltpu.VMEM((8, 128), F32),
            pltpu.VMEM((16, 8, 128), F32),
            pltpu.VMEM((16, 8, 128), F32),
            dma((6,)), dma((4,)), dma, dma((2,)), dma((2,)), dma((2,)),
            dma, dma, dma, dma, dma, dma,
            regular, regular, regular,
        ],
        compiler_params=pltpu.CompilerParams(
            collective_id=0, has_side_effects=True, vmem_limit_bytes=40 * 1024 * 1024
        ),
        cost_estimate=pl.CostEstimate(flops=10**9, bytes_accessed=12 * 10**6, transcendentals=0),
    )(
        *(
            pltpu.with_memory_space_constraint(operand, pltpu.HBM)
            for operand in (inputs.reshape(2, 4, 2, 128, 1792), out_grads, proj_in.T, proj_out.T, example_ids)
        )
    )


def solution(mesh):
    placed = (P("dp", "tensor"), P(("dp", "tensor"), None), P("tensor", None), P(), P("dp", None))
    return jax.shard_map(
        per_device, mesh=mesh, in_specs=placed, out_specs=P("dp", "tensor"), check_vma=False
    )
```

```python
import jax
import jax.numpy as jnp
from jax import lax
from jax.experimental import pallas as pl
from jax.experimental.pallas import tpu as pltpu
from jax.sharding import PartitionSpec as P

SEQ = 512
EX_DEV = 4
MESH = pl.DeviceIdType.MESH
F32 = jnp.float32
BF16 = jnp.bfloat16
NT = (((1,), (1,)), ((), ()))

CHIPS = (6, 5, 7, 2, 4, 1, 3)
TENSORS = tuple(range(15, 0, -1))
GROUPS = (10, 6, 14, 2, 9, 11, 5, 7, 13, 15, 1, 3, 8, 4, 12)


def split(x):
    high = x.astype(BF16)
    return high, (x - high.astype(F32)).astype(BF16)


def kernel(
    x_hbm, og_hbm, wi_hbm, wo_hbm, ids_hbm, out_ref,
    x_v, og_v, wi_v, wo_v, ids_v, g_v, give, take, halves, pieces, shares, mine, cols, rows,
    local_sem, x_sem, g_send, g_recv, s_send, s_recv, b_send, b_recv, c_send, last_send, col_recv, row_recv,
    x_known, z_known, all_known,
):
    dp = lax.axis_index("dp")
    tensor = lax.axis_index("tensor")
    core = lax.rem(tensor, 2)
    chip = lax.div(tensor, 2)
    y = lax.rem(chip, 4)
    z = lax.div(chip, 4)
    partner = (dp, lax.bitwise_xor(tensor, 1))

    g_reads = []
    for k in range(2):
        half = pl.ds(4096 * k, 4096)
        pair = (
            pltpu.make_async_copy(wo_hbm.at[:, half], wo_v.at[:, half], local_sem.at[2 * k]),
            pltpu.make_async_copy(og_hbm.at[:, half], og_v.at[:, half], local_sem.at[2 * k + 1]),
        )
        for copy in pair:
            copy.start()
        g_reads.append(pair)
    wi_copy = pltpu.make_async_copy(wi_hbm, wi_v, local_sem.at[4])
    ids_copy = pltpu.make_async_copy(ids_hbm, ids_v, local_sem.at[5])
    x_copies = []
    for part in range(4):
        side = lax.bitwise_xor(z, part % 2)
        owner = 1 - core if part < 2 else core
        x_copies.append(pltpu.make_async_copy(x_hbm.at[side, :, owner], x_v.at[part], x_sem.at[part]))

    barrier = pltpu.get_barrier_semaphore()
    x_peers = [(lax.bitwise_xor(dp, 4 * r), tensor) for r in (2, 1, 3)]
    z_peers = [(lax.bitwise_xor(dp, r), tensor) for r in (1, 3)]
    near = [(dp, lax.bitwise_xor(tensor, r)) for r in TENSORS] + x_peers + z_peers
    for peer in near:
        pl.semaphore_signal(barrier, inc=1, device_id=peer, device_id_type=MESH)

    sketch = []
    for k in range(2):
        for copy in g_reads[k]:
            copy.wait()
        if k == 1:
            wi_copy.start()
            ids_copy.start()
            x_copies[0].start()
            x_copies[1].start()
        half = slice(4096 * k, 4096 * (k + 1))
        sketch.append(lax.dot_general(og_v[:, half], wo_v[:, half], NT, preferred_element_type=F32))
    g_v[y] = (sketch[0] + sketch[1]).T

    pl.semaphore_wait(barrier, len(near))
    g_copies = []
    for r in CHIPS:
        copy = pltpu.make_async_remote_copy(
            src_ref=g_v.at[y], dst_ref=g_v.at[4 * (r // 4) + y],
            send_sem=g_send, recv_sem=g_recv.at[r // 4],
            device_id=(dp, 2 * lax.bitwise_xor(chip, r) + core), device_id_type=MESH,
        )
        copy.start()
        g_copies.append(copy)
    for peer in x_peers:
        pl.semaphore_signal(x_known, inc=1, device_id=peer, device_id_type=MESH)

    wi_copy.wait()
    ids_copy.wait()
    s_copies = []
    for part in range(4):
        x_copies[part].wait()
        if part < 2:
            x_copies[part + 2].start()
        sketch = lax.dot_general(
            wi_v[...], x_v[part].reshape(512, 1792), NT, preferred_element_type=F32
        )
        if part < 2:
            give[part] = sketch
            copy = pltpu.make_async_remote_copy(
                src_ref=give.at[part], dst_ref=take.at[part],
                send_sem=s_send.at[part], recv_sem=s_recv.at[part], device_id=partner, device_id_type=MESH,
            )
            copy.start()
            s_copies.append(copy)
            continue
        s_copies[part - 2].wait_recv()
        total = sketch + take[part - 2]
        side = lax.bitwise_xor(z, part % 2)
        high, low = split(total)
        lanes = slice(512 * (part - 2), 512 * (part - 1))
        halves[:64, lanes] = high
        halves[64:, lanes] = low

    pl.semaphore_wait(x_known, len(x_peers))
    for peer in z_peers:
        pl.semaphore_signal(z_known, inc=1, device_id=peer, device_id_type=MESH)

    product = None
    for side in range(2):
        count = 3 if side == 0 else 4
        arrived = g_v.at[pl.ds(0, count)]
        pltpu.make_async_copy(arrived, arrived, g_recv.at[side]).wait()
        high, low = split(jnp.concatenate([g_v[4 * side + b] for b in range(4)], axis=1))
        here = 8 * lax.bitwise_xor(z, side) + core
        ids = jnp.concatenate(
            [ids_v[:, pl.ds(pl.multiple_of((here + 2 * b) * 128, 128), 128)] for b in range(4)], axis=1
        )
        zero = jnp.zeros_like(high)
        grads = jnp.concatenate(
            [jnp.where(ids == e, part, zero) for e in range(EX_DEV) for part in (high, low)], axis=0
        )
        term = lax.dot_general(
            halves[:, 512 * side : 512 * (side + 1)], grads, NT, preferred_element_type=F32
        )
        product = term if side == 0 else product + term
    product = product[:64] + product[64:]
    lane = lax.broadcasted_iota(jnp.int32, (64, 128), 1)
    both = []
    for e in range(EX_DEV):
        term = product[:, 128 * e : 128 * (e + 1)]
        both.append(term + pltpu.roll(term, 64, 1))
    first = jnp.where(lane < 64, both[0], both[1]).reshape(8, 8, 128)
    second = jnp.where(lane < 64, both[2], both[3]).reshape(8, 8, 128)
    row8 = lax.broadcasted_iota(jnp.int32, (8, 8, 128), 1)
    even = jnp.where(row8 < 4, first, pltpu.roll(second, 4, 1))
    odd = jnp.where(row8 < 4, pltpu.roll(first, 4, 1), second)
    for u in range(8):
        pieces[2 * u] = even[u]
        pieces[2 * u + 1] = odd[u]

    for r in TENSORS:
        peer = lax.bitwise_xor(tensor, r)
        pltpu.make_async_remote_copy(
            src_ref=pieces.at[peer], dst_ref=shares.at[r], send_sem=b_send, recv_sem=b_recv,
            device_id=(dp, peer), device_id_type=MESH,
        ).start()
    pl.semaphore_wait(z_known, len(z_peers))
    for peer in z_peers:
        pl.semaphore_signal(all_known, inc=1, device_id=peer, device_id_type=MESH)
    shares[0] = pieces[tensor]
    pl.semaphore_wait(all_known, len(z_peers))
    others = shares.at[pl.ds(1, 15)]
    pltpu.make_async_copy(others, others, b_recv).wait()
    total = shares[0]
    for k in range(1, 16):
        total = total + shares[k]
    row = lax.broadcasted_iota(jnp.int32, (8, 128), 0) % 2
    lane_half = lax.broadcasted_iota(jnp.int32, (8, 128), 1) // 64
    swapped = pltpu.roll(total, 64, 1)
    piece = jnp.where(
        row == lane_half, total, jnp.where(row == 0, pltpu.roll(swapped, 7, 0), pltpu.roll(swapped, 1, 0))
    )
    mine[...] = piece

    for r in TENSORS:
        pltpu.make_async_remote_copy(
            src_ref=mine, dst_ref=rows.at[dp], send_sem=c_send, recv_sem=row_recv,
            device_id=(tensor, lax.bitwise_xor(tensor, r)), device_id_type=MESH,
        ).start()
    for r in GROUPS:
        pltpu.make_async_remote_copy(
            src_ref=mine, dst_ref=cols.at[dp], send_sem=c_send, recv_sem=col_recv,
            device_id=(lax.bitwise_xor(dp, r), tensor), device_id_type=MESH,
        ).start()
    last = pltpu.make_async_remote_copy(
        src_ref=mine, dst_ref=rows.at[dp], send_sem=last_send, recv_sem=row_recv,
        device_id=(tensor, tensor), device_id_type=MESH,
    )
    here = pltpu.make_async_copy(mine, rows.at[dp], row_recv)

    @pl.when(tensor != dp)
    def _():
        last.start()

    @pl.when(tensor == dp)
    def _():
        here.start()

    cols[dp] = piece
    others = cols.at[pl.ds(0, 15)]
    pltpu.make_async_copy(others, others, col_recv).wait()
    pltpu.make_async_copy(rows, rows, row_recv).wait()

    r2 = rows[...].reshape(128, 128).T
    c2 = cols[...].reshape(128, 128)
    r_bit = (lax.broadcasted_iota(jnp.int32, (128, 128), 1) // 2) % 2
    c_bit = (lax.broadcasted_iota(jnp.int32, (128, 128), 0) // 2) % 2
    zero = jnp.zeros_like(r2)
    left = jnp.concatenate([jnp.where(r_bit == 0, r2, zero), jnp.where(r_bit == 1, r2, zero)], axis=0)
    right = jnp.concatenate(
        [jnp.where(c_bit == 0, c2, pltpu.roll(c2, 2, 0)), jnp.where(c_bit == 1, c2, pltpu.roll(c2, 126, 0))], axis=1
    )
    lh, ll = split(left)
    rh, rl = split(right)
    dot = lambda a, b: jnp.dot(a, b, preferred_element_type=F32)
    out_ref[...] = dot(
        jnp.concatenate([lh, ll, lh], axis=1), jnp.concatenate([rl, rh, rh], axis=0)
    ) * (1.0 / (64 * SEQ))

    for copy in s_copies:
        copy.wait_send()
    sent = g_v.at[pl.ds(0, 7)]
    pltpu.make_async_copy(sent, sent, g_send).wait()
    sent = shares.at[pl.ds(0, 15)]
    pltpu.make_async_copy(sent, sent, b_send).wait()
    sent = cols.at[pl.ds(0, 15)]
    pltpu.make_async_copy(sent, sent, c_send).wait()
    pltpu.make_async_copy(sent, sent, c_send).wait()

    @pl.when(tensor != dp)
    def _():
        last.wait_send()


def per_device(inputs, out_grads, proj_in, proj_out, example_ids):
    hbm = pl.BlockSpec(memory_space=pltpu.HBM)
    dma = pltpu.SemaphoreType.DMA
    regular = pltpu.SemaphoreType.REGULAR
    return pl.pallas_call(
        kernel,
        out_shape=pltpu.VMEM((256, 256), F32),
        in_specs=[hbm] * 5,
        out_specs=pl.BlockSpec(memory_space=pltpu.VMEM),
        scratch_shapes=[
            pltpu.VMEM((4, 4, 128, 1792), BF16),
            pltpu.VMEM((128, 8192), BF16),
            pltpu.VMEM((64, 1792), BF16),
            pltpu.VMEM((64, 8192), BF16),
            pltpu.VMEM((1, 2048), jnp.int32),
            pltpu.VMEM((8, 64, 128), F32),
            pltpu.VMEM((2, 64, 512), F32),
            pltpu.VMEM((2, 64, 512), F32),
            pltpu.VMEM((128, 1024), BF16),
            pltpu.VMEM((16, 8, 128), F32),
            pltpu.VMEM((16, 8, 128), F32),
            pltpu.VMEM((8, 128), F32),
            pltpu.VMEM((16, 8, 128), F32),
            pltpu.VMEM((16, 8, 128), F32),
            dma((6,)), dma((4,)), dma, dma((2,)), dma((2,)), dma((2,)),
            dma, dma, dma, dma, dma, dma,
            regular, regular, regular,
        ],
        compiler_params=pltpu.CompilerParams(
            collective_id=0, has_side_effects=True, vmem_limit_bytes=40 * 1024 * 1024
        ),
        cost_estimate=pl.CostEstimate(flops=10**9, bytes_accessed=12 * 10**6, transcendentals=0),
    )(
        *(
            pltpu.with_memory_space_constraint(operand, pltpu.HBM)
            for operand in (inputs.reshape(2, 4, 2, 128, 1792), out_grads, proj_in.T, proj_out.T, example_ids)
        )
    )


def solution(mesh):
    placed = (P("dp", "tensor"), P(("dp", "tensor"), None), P("tensor", None), P(), P("dp", None))
    return jax.shard_map(
        per_device, mesh=mesh, in_specs=placed, out_specs=P("dp", "tensor"), check_vma=False
    )
```

```python
import jax
import jax.numpy as jnp
from jax import lax
from jax.experimental import pallas as pl
from jax.experimental.pallas import tpu as pltpu
from jax.sharding import PartitionSpec as P

SEQ = 512
EX_DEV = 4
MESH = pl.DeviceIdType.MESH
F32 = jnp.float32
BF16 = jnp.bfloat16
NT = (((1,), (1,)), ((), ()))

CHIPS = (6, 5, 7, 2, 4, 1, 3)
TENSORS = tuple(range(15, 0, -1))
GROUPS = (10, 6, 14, 2, 9, 11, 5, 7, 13, 15, 1, 3, 8, 4, 12)


def split(x):
    high = x.astype(BF16)
    return high, (x - high.astype(F32)).astype(BF16)


def kernel(
    x_hbm, og_hbm, wi_hbm, wo_hbm, ids_hbm, out_ref,
    x_v, og_v, wi_v, wo_v, ids_v, g_v, give, take, halves, pieces, shares, mine, cols, rows, final,
    local_sem, x_sem, g_send, g_recv, s_send, s_recv, b_send, b_recv, c_send, last_send, col_recv, row_recv,
    x_known, z_known, all_known,
):
    dp = lax.axis_index("dp")
    tensor = lax.axis_index("tensor")
    core = lax.rem(tensor, 2)
    chip = lax.div(tensor, 2)
    y = lax.rem(chip, 4)
    z = lax.div(chip, 4)
    partner = (dp, lax.bitwise_xor(tensor, 1))

    g_reads = []
    for k in range(2):
        half = pl.ds(4096 * k, 4096)
        pair = (
            pltpu.make_async_copy(wo_hbm.at[:, half], wo_v.at[:, half], local_sem.at[2 * k]),
            pltpu.make_async_copy(og_hbm.at[:, half], og_v.at[:, half], local_sem.at[2 * k + 1]),
        )
        for copy in pair:
            copy.start()
        g_reads.append(pair)
    wi_copy = pltpu.make_async_copy(wi_hbm, wi_v, local_sem.at[4])
    ids_copy = pltpu.make_async_copy(ids_hbm, ids_v, local_sem.at[5])
    x_copies = []
    for part in range(4):
        side = lax.bitwise_xor(z, part % 2)
        owner = 1 - core if part < 2 else core
        x_copies.append(pltpu.make_async_copy(x_hbm.at[side, :, owner], x_v.at[part], x_sem.at[part]))

    barrier = pltpu.get_barrier_semaphore()
    x_peers = [(lax.bitwise_xor(dp, 4 * r), tensor) for r in (2, 1, 3)]
    z_peers = [(lax.bitwise_xor(dp, r), tensor) for r in (1, 3)]
    near = [(dp, lax.bitwise_xor(tensor, r)) for r in TENSORS] + x_peers + z_peers
    for peer in near:
        pl.semaphore_signal(barrier, inc=1, device_id=peer, device_id_type=MESH)

    sketch = []
    for k in range(2):
        for copy in g_reads[k]:
            copy.wait()
        if k == 1:
            wi_copy.start()
            ids_copy.start()
            x_copies[0].start()
            x_copies[1].start()
        half = slice(4096 * k, 4096 * (k + 1))
        sketch.append(lax.dot_general(og_v[:, half], wo_v[:, half], NT, preferred_element_type=F32))
    g_v[y] = (sketch[0] + sketch[1]).T

    pl.semaphore_wait(barrier, len(near))
    g_copies = []
    for r in CHIPS:
        copy = pltpu.make_async_remote_copy(
            src_ref=g_v.at[y], dst_ref=g_v.at[4 * (r // 4) + y],
            send_sem=g_send, recv_sem=g_recv.at[r // 4],
            device_id=(dp, 2 * lax.bitwise_xor(chip, r) + core), device_id_type=MESH,
        )
        copy.start()
        g_copies.append(copy)
    for peer in x_peers:
        pl.semaphore_signal(x_known, inc=1, device_id=peer, device_id_type=MESH)

    wi_copy.wait()
    ids_copy.wait()
    s_copies = []
    for part in range(4):
        x_copies[part].wait()
        if part < 2:
            x_copies[part + 2].start()
        sketch = lax.dot_general(
            wi_v[...], x_v[part].reshape(512, 1792), NT, preferred_element_type=F32
        )
        if part < 2:
            give[part] = sketch
            copy = pltpu.make_async_remote_copy(
                src_ref=give.at[part], dst_ref=take.at[part],
                send_sem=s_send.at[part], recv_sem=s_recv.at[part], device_id=partner, device_id_type=MESH,
            )
            copy.start()
            s_copies.append(copy)
            continue
        s_copies[part - 2].wait_recv()
        total = sketch + take[part - 2]
        side = lax.bitwise_xor(z, part % 2)
        high, low = split(total)
        lanes = slice(512 * (part - 2), 512 * (part - 1))
        halves[:64, lanes] = high
        halves[64:, lanes] = low

    pl.semaphore_wait(x_known, len(x_peers))
    for peer in z_peers:
        pl.semaphore_signal(z_known, inc=1, device_id=peer, device_id_type=MESH)

    product = None
    for side in range(2):
        count = 3 if side == 0 else 4
        arrived = g_v.at[pl.ds(0, count)]
        pltpu.make_async_copy(arrived, arrived, g_recv.at[side]).wait()
        high, low = split(jnp.concatenate([g_v[4 * side + b] for b in range(4)], axis=1))
        here = 8 * lax.bitwise_xor(z, side) + core
        ids = jnp.concatenate(
            [ids_v[:, pl.ds(pl.multiple_of((here + 2 * b) * 128, 128), 128)] for b in range(4)], axis=1
        )
        zero = jnp.zeros_like(high)
        grads = jnp.concatenate(
            [jnp.where(ids == e, part, zero) for e in range(EX_DEV) for part in (high, low)], axis=0
        )
        term = lax.dot_general(
            halves[:, 512 * side : 512 * (side + 1)], grads, NT, preferred_element_type=F32
        )
        product = term if side == 0 else product + term
    product = product[:64] + product[64:]
    lane = lax.broadcasted_iota(jnp.int32, (64, 128), 1)
    both = []
    for e in range(EX_DEV):
        term = product[:, 128 * e : 128 * (e + 1)]
        both.append(term + pltpu.roll(term, 64, 1))
    first = jnp.where(lane < 64, both[0], both[1]).reshape(8, 8, 128)
    second = jnp.where(lane < 64, both[2], both[3]).reshape(8, 8, 128)
    row8 = lax.broadcasted_iota(jnp.int32, (8, 8, 128), 1)
    even = jnp.where(row8 < 4, first, pltpu.roll(second, 4, 1))
    odd = jnp.where(row8 < 4, pltpu.roll(first, 4, 1), second)
    for u in range(8):
        pieces[2 * u] = even[u]
        pieces[2 * u + 1] = odd[u]

    for r in TENSORS:
        peer = lax.bitwise_xor(tensor, r)
        pltpu.make_async_remote_copy(
            src_ref=pieces.at[peer], dst_ref=shares.at[r], send_sem=b_send, recv_sem=b_recv,
            device_id=(dp, peer), device_id_type=MESH,
        ).start()
    pl.semaphore_wait(z_known, len(z_peers))
    for peer in z_peers:
        pl.semaphore_signal(all_known, inc=1, device_id=peer, device_id_type=MESH)
    shares[0] = pieces[tensor]
    pl.semaphore_wait(all_known, len(z_peers))
    others = shares.at[pl.ds(1, 15)]
    pltpu.make_async_copy(others, others, b_recv).wait()
    total = shares[0]
    for k in range(1, 16):
        total = total + shares[k]
    row = lax.broadcasted_iota(jnp.int32, (8, 128), 0) % 2
    lane_half = lax.broadcasted_iota(jnp.int32, (8, 128), 1) // 64
    swapped = pltpu.roll(total, 64, 1)
    piece = jnp.where(
        row == lane_half, total, jnp.where(row == 0, pltpu.roll(swapped, 7, 0), pltpu.roll(swapped, 1, 0))
    )
    mine[...] = piece

    for r in TENSORS:
        pltpu.make_async_remote_copy(
            src_ref=mine, dst_ref=rows.at[dp], send_sem=c_send, recv_sem=row_recv,
            device_id=(tensor, lax.bitwise_xor(tensor, r)), device_id_type=MESH,
        ).start()
    for r in GROUPS:
        pltpu.make_async_remote_copy(
            src_ref=mine, dst_ref=cols.at[dp], send_sem=c_send, recv_sem=col_recv,
            device_id=(lax.bitwise_xor(dp, r), tensor), device_id_type=MESH,
        ).start()
    last = pltpu.make_async_remote_copy(
        src_ref=mine, dst_ref=rows.at[dp], send_sem=last_send, recv_sem=row_recv,
        device_id=(tensor, tensor), device_id_type=MESH,
    )
    here = pltpu.make_async_copy(mine, rows.at[dp], row_recv)

    @pl.when(tensor != dp)
    def _():
        last.start()

    @pl.when(tensor == dp)
    def _():
        here.start()

    cols[dp] = piece
    others = cols.at[pl.ds(0, 15)]
    pltpu.make_async_copy(others, others, col_recv).wait()
    c2 = cols[...].reshape(128, 128)
    c_bit = (lax.broadcasted_iota(jnp.int32, (128, 128), 0) // 2) % 2
    right = jnp.concatenate(
        [jnp.where(c_bit == 0, c2, pltpu.roll(c2, 2, 0)), jnp.where(c_bit == 1, c2, pltpu.roll(c2, 126, 0))], axis=1
    )
    rh, rl = split(right)
    final[...] = jnp.concatenate([rl, rh, rh], axis=0)
    pltpu.make_async_copy(rows, rows, row_recv).wait()
    r2 = rows[...].reshape(128, 128).T
    r_bit = (lax.broadcasted_iota(jnp.int32, (128, 128), 1) // 2) % 2
    zero = jnp.zeros_like(r2)
    left = jnp.concatenate([jnp.where(r_bit == 0, r2, zero), jnp.where(r_bit == 1, r2, zero)], axis=0)
    lh, ll = split(left)
    out_ref[...] = jnp.dot(
        jnp.concatenate([lh, ll, lh], axis=1), final[...], preferred_element_type=F32
    ) * (1.0 / (64 * SEQ))

    for copy in s_copies:
        copy.wait_send()
    sent = g_v.at[pl.ds(0, 7)]
    pltpu.make_async_copy(sent, sent, g_send).wait()
    sent = shares.at[pl.ds(0, 15)]
    pltpu.make_async_copy(sent, sent, b_send).wait()
    sent = cols.at[pl.ds(0, 15)]
    pltpu.make_async_copy(sent, sent, c_send).wait()
    pltpu.make_async_copy(sent, sent, c_send).wait()

    @pl.when(tensor != dp)
    def _():
        last.wait_send()


def per_device(inputs, out_grads, proj_in, proj_out, example_ids):
    hbm = pl.BlockSpec(memory_space=pltpu.HBM)
    dma = pltpu.SemaphoreType.DMA
    regular = pltpu.SemaphoreType.REGULAR
    return pl.pallas_call(
        kernel,
        out_shape=pltpu.VMEM((256, 256), F32),
        in_specs=[hbm] * 5,
        out_specs=pl.BlockSpec(memory_space=pltpu.VMEM),
        scratch_shapes=[
            pltpu.VMEM((4, 4, 128, 1792), BF16),
            pltpu.VMEM((128, 8192), BF16),
            pltpu.VMEM((64, 1792), BF16),
            pltpu.VMEM((64, 8192), BF16),
            pltpu.VMEM((1, 2048), jnp.int32),
            pltpu.VMEM((8, 64, 128), F32),
            pltpu.VMEM((2, 64, 512), F32),
            pltpu.VMEM((2, 64, 512), F32),
            pltpu.VMEM((128, 1024), BF16),
            pltpu.VMEM((16, 8, 128), F32),
            pltpu.VMEM((16, 8, 128), F32),
            pltpu.VMEM((8, 128), F32),
            pltpu.VMEM((16, 8, 128), F32),
            pltpu.VMEM((16, 8, 128), F32),
            pltpu.VMEM((384, 256), BF16),
            dma((6,)), dma((4,)), dma, dma((2,)), dma((2,)), dma((2,)),
            dma, dma, dma, dma, dma, dma,
            regular, regular, regular,
        ],
        compiler_params=pltpu.CompilerParams(
            collective_id=0, has_side_effects=True, vmem_limit_bytes=40 * 1024 * 1024
        ),
        cost_estimate=pl.CostEstimate(flops=10**9, bytes_accessed=12 * 10**6, transcendentals=0),
    )(
        *(
            pltpu.with_memory_space_constraint(operand, pltpu.HBM)
            for operand in (inputs.reshape(2, 4, 2, 128, 1792), out_grads, proj_in.T, proj_out.T, example_ids)
        )
    )


def solution(mesh):
    placed = (P("dp", "tensor"), P(("dp", "tensor"), None), P("tensor", None), P(), P("dp", None))
    return jax.shard_map(
        per_device, mesh=mesh, in_specs=placed, out_specs=P("dp", "tensor"), check_vma=False
    )
```

```python
import jax
import jax.numpy as jnp
from jax import lax
from jax.experimental import pallas as pl
from jax.experimental.pallas import tpu as pltpu
from jax.sharding import PartitionSpec as P

SEQ = 512
EX_DEV = 4
MESH = pl.DeviceIdType.MESH
F32 = jnp.float32
BF16 = jnp.bfloat16
NT = (((1,), (1,)), ((), ()))

CHIPS = (6, 5, 7, 2, 4, 1, 3)
TENSORS = tuple(range(15, 0, -1))
GROUPS = (10, 6, 14, 2, 9, 11, 5, 7, 13, 15, 1, 3, 8, 4, 12)


def split(x):
    high = x.astype(BF16)
    return high, (x - high.astype(F32)).astype(BF16)


def kernel(
    x_hbm, og_hbm, wi_hbm, wo_hbm, ids_hbm, out_ref,
    x_v, og_v, wi_v, wo_v, ids_v, g_v, give, take, halves, pieces, shares, mine, cols, rows, final,
    local_sem, x_sem, g_send, g_recv, s_send, s_recv, b_send, b_recv, c_send, last_send, col_recv, row_recv,
    x_known, z_known, all_known,
):
    dp = lax.axis_index("dp")
    tensor = lax.axis_index("tensor")
    core = lax.rem(tensor, 2)
    chip = lax.div(tensor, 2)
    y = lax.rem(chip, 4)
    z = lax.div(chip, 4)
    partner = (dp, lax.bitwise_xor(tensor, 1))

    g_reads = []
    for k in range(2):
        half = pl.ds(4096 * k, 4096)
        pair = (
            pltpu.make_async_copy(wo_hbm.at[:, half], wo_v.at[:, half], local_sem.at[2 * k]),
            pltpu.make_async_copy(og_hbm.at[:, half], og_v.at[:, half], local_sem.at[2 * k + 1]),
        )
        for copy in pair:
            copy.start()
        g_reads.append(pair)
    wi_copy = pltpu.make_async_copy(wi_hbm, wi_v, local_sem.at[4])
    ids_copy = pltpu.make_async_copy(ids_hbm, ids_v, local_sem.at[5])
    x_copies = []
    for part in range(4):
        side = lax.bitwise_xor(z, part % 2)
        owner = 1 - core if part < 2 else core
        x_copies.append(pltpu.make_async_copy(x_hbm.at[side, :, owner], x_v.at[part], x_sem.at[part]))

    barrier = pltpu.get_barrier_semaphore()
    x_peers = [(lax.bitwise_xor(dp, 4 * r), tensor) for r in (2, 1, 3)]
    z_peers = [(lax.bitwise_xor(dp, r), tensor) for r in (1, 3)]
    near = [(dp, lax.bitwise_xor(tensor, r)) for r in TENSORS] + x_peers + z_peers
    for peer in near:
        pl.semaphore_signal(barrier, inc=1, device_id=peer, device_id_type=MESH)

    sketch = []
    for k in range(2):
        for copy in g_reads[k]:
            copy.wait()
        if k == 1:
            wi_copy.start()
            ids_copy.start()
            x_copies[0].start()
            x_copies[1].start()
        half = slice(4096 * k, 4096 * (k + 1))
        sketch.append(lax.dot_general(og_v[:, half], wo_v[:, half], NT, preferred_element_type=F32))
    g_v[y] = (sketch[0] + sketch[1]).T

    pl.semaphore_wait(barrier, len(near))
    g_copies = []
    for r in CHIPS:
        copy = pltpu.make_async_remote_copy(
            src_ref=g_v.at[y], dst_ref=g_v.at[4 * (r // 4) + y],
            send_sem=g_send, recv_sem=g_recv.at[r // 4],
            device_id=(dp, 2 * lax.bitwise_xor(chip, r) + core), device_id_type=MESH,
        )
        copy.start()
        g_copies.append(copy)
    for peer in x_peers:
        pl.semaphore_signal(x_known, inc=1, device_id=peer, device_id_type=MESH)

    wi_copy.wait()
    ids_copy.wait()
    s_copies = []
    for part in range(4):
        x_copies[part].wait()
        if part < 2:
            x_copies[part + 2].start()
        sketch = lax.dot_general(
            wi_v[...], x_v[part].reshape(512, 1792), NT, preferred_element_type=F32
        )
        if part < 2:
            give[part] = sketch
            copy = pltpu.make_async_remote_copy(
                src_ref=give.at[part], dst_ref=take.at[part],
                send_sem=s_send.at[part], recv_sem=s_recv.at[part], device_id=partner, device_id_type=MESH,
            )
            copy.start()
            s_copies.append(copy)
            continue
        s_copies[part - 2].wait_recv()
        total = sketch + take[part - 2]
        side = lax.bitwise_xor(z, part % 2)
        high, low = split(total)
        lanes = slice(512 * (part - 2), 512 * (part - 1))
        halves[:64, lanes] = high
        halves[64:, lanes] = low

    pl.semaphore_wait(x_known, len(x_peers))
    for peer in z_peers:
        pl.semaphore_signal(z_known, inc=1, device_id=peer, device_id_type=MESH)

    product = None
    for side in range(2):
        count = 3 if side == 0 else 4
        arrived = g_v.at[pl.ds(0, count)]
        pltpu.make_async_copy(arrived, arrived, g_recv.at[side]).wait()
        high, low = split(jnp.concatenate([g_v[4 * side + b] for b in range(4)], axis=1))
        here = 8 * lax.bitwise_xor(z, side) + core
        ids = jnp.concatenate(
            [ids_v[:, pl.ds(pl.multiple_of((here + 2 * b) * 128, 128), 128)] for b in range(4)], axis=1
        )
        zero = jnp.zeros_like(high)
        grads = jnp.concatenate(
            [jnp.where(ids == e, part, zero) for e in range(EX_DEV) for part in (high, low)], axis=0
        )
        term = lax.dot_general(
            halves[:, 512 * side : 512 * (side + 1)], grads, NT, preferred_element_type=F32
        )
        product = term if side == 0 else product + term
    product = product[:64] + product[64:]
    lane = lax.broadcasted_iota(jnp.int32, (64, 128), 1)
    both = []
    for e in range(EX_DEV):
        term = product[:, 128 * e : 128 * (e + 1)]
        both.append(term + pltpu.roll(term, 64, 1))
    first = jnp.where(lane < 64, both[0], both[1]).reshape(8, 8, 128)
    second = jnp.where(lane < 64, both[2], both[3]).reshape(8, 8, 128)
    row8 = lax.broadcasted_iota(jnp.int32, (8, 8, 128), 1)
    even = jnp.where(row8 < 4, first, pltpu.roll(second, 4, 1))
    odd = jnp.where(row8 < 4, pltpu.roll(first, 4, 1), second)
    for u in range(8):
        pieces[2 * u] = even[u]
        pieces[2 * u + 1] = odd[u]

    for r in TENSORS:
        peer = lax.bitwise_xor(tensor, r)
        pltpu.make_async_remote_copy(
            src_ref=pieces.at[peer], dst_ref=shares.at[r], send_sem=b_send, recv_sem=b_recv,
            device_id=(dp, peer), device_id_type=MESH,
        ).start()
    pl.semaphore_wait(z_known, len(z_peers))
    for peer in z_peers:
        pl.semaphore_signal(all_known, inc=1, device_id=peer, device_id_type=MESH)
    shares[0] = pieces[tensor]
    pl.semaphore_wait(all_known, len(z_peers))
    others = shares.at[pl.ds(1, 15)]
    pltpu.make_async_copy(others, others, b_recv).wait()
    total = shares[0]
    for k in range(1, 16):
        total = total + shares[k]
    row = lax.broadcasted_iota(jnp.int32, (8, 128), 0) % 2
    lane_half = lax.broadcasted_iota(jnp.int32, (8, 128), 1) // 64
    swapped = pltpu.roll(total, 64, 1)
    piece = jnp.where(
        row == lane_half, total, jnp.where(row == 0, pltpu.roll(swapped, 7, 0), pltpu.roll(swapped, 1, 0))
    )
    mine[...] = piece

    for r in TENSORS:
        pltpu.make_async_remote_copy(
            src_ref=mine, dst_ref=rows.at[dp], send_sem=c_send, recv_sem=row_recv,
            device_id=(tensor, lax.bitwise_xor(tensor, r)), device_id_type=MESH,
        ).start()
    last = pltpu.make_async_remote_copy(
        src_ref=mine, dst_ref=rows.at[dp], send_sem=last_send, recv_sem=row_recv,
        device_id=(tensor, tensor), device_id_type=MESH,
    )
    here = pltpu.make_async_copy(mine, rows.at[dp], row_recv)

    @pl.when(tensor != dp)
    def _():
        last.start()

    @pl.when(tensor == dp)
    def _():
        here.start()

    for r in GROUPS:
        pltpu.make_async_remote_copy(
            src_ref=mine, dst_ref=cols.at[dp], send_sem=c_send, recv_sem=col_recv,
            device_id=(lax.bitwise_xor(dp, r), tensor), device_id_type=MESH,
        ).start()
    cols[dp] = piece
    others = cols.at[pl.ds(0, 15)]
    pltpu.make_async_copy(others, others, col_recv).wait()
    c2 = cols[...].reshape(128, 128)
    c_bit = (lax.broadcasted_iota(jnp.int32, (128, 128), 0) // 2) % 2
    right = jnp.concatenate(
        [jnp.where(c_bit == 0, c2, pltpu.roll(c2, 2, 0)), jnp.where(c_bit == 1, c2, pltpu.roll(c2, 126, 0))], axis=1
    )
    rh, rl = split(right)
    final[...] = jnp.concatenate([rl, rh, rh], axis=0)
    pltpu.make_async_copy(rows, rows, row_recv).wait()
    r2 = rows[...].reshape(128, 128).T
    r_bit = (lax.broadcasted_iota(jnp.int32, (128, 128), 1) // 2) % 2
    zero = jnp.zeros_like(r2)
    left = jnp.concatenate([jnp.where(r_bit == 0, r2, zero), jnp.where(r_bit == 1, r2, zero)], axis=0)
    lh, ll = split(left)
    out_ref[...] = jnp.dot(
        jnp.concatenate([lh, ll, lh], axis=1), final[...], preferred_element_type=F32
    ) * (1.0 / (64 * SEQ))

    for copy in s_copies:
        copy.wait_send()
    sent = g_v.at[pl.ds(0, 7)]
    pltpu.make_async_copy(sent, sent, g_send).wait()
    sent = shares.at[pl.ds(0, 15)]
    pltpu.make_async_copy(sent, sent, b_send).wait()
    sent = cols.at[pl.ds(0, 15)]
    pltpu.make_async_copy(sent, sent, c_send).wait()
    pltpu.make_async_copy(sent, sent, c_send).wait()

    @pl.when(tensor != dp)
    def _():
        last.wait_send()


def per_device(inputs, out_grads, proj_in, proj_out, example_ids):
    hbm = pl.BlockSpec(memory_space=pltpu.HBM)
    dma = pltpu.SemaphoreType.DMA
    regular = pltpu.SemaphoreType.REGULAR
    return pl.pallas_call(
        kernel,
        out_shape=pltpu.VMEM((256, 256), F32),
        in_specs=[hbm] * 5,
        out_specs=pl.BlockSpec(memory_space=pltpu.VMEM),
        scratch_shapes=[
            pltpu.VMEM((4, 4, 128, 1792), BF16),
            pltpu.VMEM((128, 8192), BF16),
            pltpu.VMEM((64, 1792), BF16),
            pltpu.VMEM((64, 8192), BF16),
            pltpu.VMEM((1, 2048), jnp.int32),
            pltpu.VMEM((8, 64, 128), F32),
            pltpu.VMEM((2, 64, 512), F32),
            pltpu.VMEM((2, 64, 512), F32),
            pltpu.VMEM((128, 1024), BF16),
            pltpu.VMEM((16, 8, 128), F32),
            pltpu.VMEM((16, 8, 128), F32),
            pltpu.VMEM((8, 128), F32),
            pltpu.VMEM((16, 8, 128), F32),
            pltpu.VMEM((16, 8, 128), F32),
            pltpu.VMEM((384, 256), BF16),
            dma((6,)), dma((4,)), dma, dma((2,)), dma((2,)), dma((2,)),
            dma, dma, dma, dma, dma, dma,
            regular, regular, regular,
        ],
        compiler_params=pltpu.CompilerParams(
            collective_id=0, has_side_effects=True, vmem_limit_bytes=40 * 1024 * 1024
        ),
        cost_estimate=pl.CostEstimate(flops=10**9, bytes_accessed=12 * 10**6, transcendentals=0),
    )(
        *(
            pltpu.with_memory_space_constraint(operand, pltpu.HBM)
            for operand in (inputs.reshape(2, 4, 2, 128, 1792), out_grads, proj_in.T, proj_out.T, example_ids)
        )
    )


def solution(mesh):
    placed = (P("dp", "tensor"), P(("dp", "tensor"), None), P("tensor", None), P(), P("dp", None))
    return jax.shard_map(
        per_device, mesh=mesh, in_specs=placed, out_specs=P("dp", "tensor"), check_vma=False
    )
```
